1024 devices in a mesh: outer: 32 (over x, z_lo), inner: 32 (over y, z_hi, core).
Axes of the slice: x: 4, y: 4, z: 32 (z_hi: 4, z_lo: 8; z = z_hi * 8 + z_lo), core: 2. Of those that a mesh axis runs over, the one named last changes fastest.
Arguments:
- out_grad: bfloat16 [196608, 8192], P(('outer', 'inner')), may hold values from -6 to 6
- hidden: bfloat16 [196608, 128], P(('outer', 'inner')), may hold values from -0.0546875 to 0.0546875
- weight: bfloat16 [128, 8192], P(None, 'inner'), may hold values from -0.0625 to 0.0625
- first_exponent: int32 [131072, 64], P(('outer', 'inner')), may hold values from -16 to -8
- second_exponent: int32 [4096, 64], P('outer', 'inner'), may hold values from -14 to -6
Outputs:
- hidden_grad: bfloat16 [196608, 128], P(('outer', 'inner'))
- weight_grad: float32 [128, 8192], P('outer', 'inner')
The draws below stay inside these ranges and needn't reach their ends.
All inputs are finite; a program needn't handle non-finite values.
Results may differ from the reference program's by a relative error of at most 0.01.
Values may be sent and summed in bfloat16 or wider, within the bound.
No kernel may reach another device: no remote copies, remote signals or barrier semaphores. Data moves between devices by JAX's collectives and lax.ppermute only.
A program may use at most 32 MiB of HBM per device.

```python
import jax
import jax.numpy as jnp
from jax import lax

D = 8192
BUCKET = 128
TOK_DEV = 192
TOKENS = 196608
N_OUTER = 32
N_INNER = 32


def set_ends(array, stream_key, least, largest):
    dims = array.shape
    spot = [jax.random.randint(jax.random.fold_in(stream_key, axis), (), 0, dims[axis]) for axis in range(len(dims))]
    array = array.at[tuple(spot)].set(least)
    longest = dims.index(max(dims))
    spot[longest] = (spot[longest] + 1) % dims[longest]
    return array.at[tuple(spot)].set(largest)


def raised(array, own_key, source, target, parts, factor):
    def block_of(dim):
        return (jnp.arange(array.shape[dim]) // (array.shape[dim] // parts)).reshape((-1,) + (1,) * (array.ndim - 1 - dim))

    first = jax.random.permutation(own_key, parts)[block_of(target)]
    far = (block_of(target) + parts // 2) % parts
    return jnp.where((block_of(source) == first) | (block_of(source) == far), factor * array, array)


def block_levels(stream_key, extent, pieces, low, top_value):
    level = 1.0
    for dim, shards_of in pieces:
        draws = jax.random.uniform(jax.random.fold_in(jax.random.fold_in(stream_key, 6), dim), (shards_of,), jnp.float32, low / len(pieces), top_value / len(pieces))
        level = level * jnp.repeat(jnp.exp(draws), extent[dim] // shards_of).reshape((-1,) + (1,) * (len(extent) - 1 - dim))
    return level


def normal_values(own_key, shape, spread, bound, cuts=(), kind=jnp.bfloat16):
    values = spread * jax.random.normal(own_key, shape, jnp.float32)
    if cuts:
        values = values * block_levels(own_key, shape, cuts, -0.22, 0.18)
    return jnp.clip(values, -bound, bound).astype(kind)


def gaussian_with(key, extent, scale, reach, pieces, heavy, held_as=jnp.bfloat16):
    drawn = scale * jax.random.normal(key, extent, jnp.float32)
    if pieces:
        drawn = drawn * block_levels(key, extent, pieces, -0.22, 0.18)
    return jnp.clip(raised(drawn, jax.random.fold_in(key, 3), *heavy), -reach, reach).astype(held_as)


def setup_inputs(seed: int = 0) -> dict:
    keys = jax.random.split(jax.random.key(seed), 6)
    out_grad = normal_values(keys[0], (TOKENS, D), 1.0, 6.0, ((0, 1024),))
    hidden = gaussian_with(keys[1], (TOKENS, BUCKET), ((TOK_DEV * N_OUTER * N_INNER) ** -0.5), 0.0546875, ((0, 1024),), (0, 1, 128, 5.5))
    weight = normal_values(keys[2], (BUCKET, D), D ** -0.5, 0.0625, ((1, 32),))
    first_exponent = set_ends(jax.random.randint(keys[3], (BUCKET * N_OUTER * N_INNER, D // 128), -16, -7), jax.random.fold_in(keys[3], 1), -16, (-7) - 1).astype(jnp.int32)
    second_exponent = set_ends(jax.random.randint(keys[4], (BUCKET * N_OUTER, D // 128), -14, -5), jax.random.fold_in(keys[4], 1), -14, (-5) - 1).astype(jnp.int32)
    return dict(out_grad=out_grad, hidden=hidden, weight=weight, first_exponent=first_exponent, second_exponent=second_exponent)


def quantize(values, exponents):
    shape = values.shape
    scale = jnp.exp2(exponents.astype(jnp.float32))[..., None]
    blocks = values.reshape(shape[:-1] + (shape[-1] // 128, 128))
    clipped = jnp.clip(blocks / scale, -448.0, 448.0).astype(jnp.bfloat16)
    return (clipped.astype(jnp.float32) * scale).astype(jnp.bfloat16).reshape(shape)


def reference(out_grad, hidden, weight, first_exponent, second_exponent):
    hidden_grad = jnp.dot(out_grad, weight.T, preferred_element_type=jnp.float32).astype(jnp.bfloat16)
    grads = out_grad.reshape(N_OUTER, N_INNER, TOK_DEV, D)
    acts = hidden.reshape(N_OUTER, N_INNER, TOK_DEV, BUCKET)
    firsts = first_exponent.reshape(N_OUTER, N_INNER, BUCKET, D // 128)
    seconds = second_exponent.reshape(N_OUTER, BUCKET, D // 128)

    def step(total, items):
        grad_block, act_block, first_part, second_part = items
        local_grad = jnp.einsum("itr,itd->ird", act_block.astype(jnp.float32), grad_block.astype(jnp.float32))
        group_sum = jnp.sum(quantize(local_grad, first_part).astype(jnp.float32), axis=0)
        return total + quantize(group_sum, second_part).astype(jnp.float32), None

    start = jnp.zeros((BUCKET, D), jnp.float32)
    weight_grad, unused = lax.scan(step, start, (grads, acts, firsts, seconds))
    return hidden_grad, weight_grad
```

```python
import jax
import jax.numpy as jnp
from jax import lax
from jax.experimental import pallas as pl
from jax.experimental.pallas import tpu as pltpu
from jax.sharding import Mesh, PartitionSpec as P

SIZES = {"x": 4, "zl": 8, "y": 4, "zh": 4, "c": 2}
AXES = tuple(SIZES)
OUTER = ("x", "zl")
LIMIT = 448.0


def shifted(value, axis, k):
    n = SIZES[axis]
    return lax.ppermute(value, axis, [(i, (i - k) % n) for i in range(n)])


def sent(value, axis, k):
    return shifted(value, axis, -k)


def grad_kernel(pos, hid, og_own, og_oth, e1, own, oth):
    j, c = pl.program_id(0), pos[0]
    bound = (jnp.left_shift(1, e1[...] + 16).astype(jnp.float32) * (LIMIT * 2.0**-16)).astype(jnp.bfloat16)
    rows = lax.broadcasted_iota(jnp.int32, (64, 256), 0)
    lanes = lax.broadcasted_iota(jnp.int32, (64, 256), 1) // 128
    for core, og, out in ((c, og_own, own), (1 - c, og_oth, oth)):
        pick = (rows == (2 * j + core) * 2 + lanes).astype(jnp.bfloat16)
        limit = jnp.dot(bound, pick, preferred_element_type=jnp.float32)
        local = lax.dot_general(hid[...], og[...], (((0,), (0,)), ((), ())), preferred_element_type=jnp.float32)
        out[0] = jnp.clip(local, -limit, limit).astype(jnp.bfloat16)


def local_grads(pos, hidden, out_grad, e1):
    block = jax.ShapeDtypeStruct((16, 128, 256), jnp.bfloat16)
    return pl.pallas_call(
        grad_kernel,
        grid_spec=pltpu.PrefetchScalarGridSpec(
            num_scalar_prefetch=1,
            grid=(16,),
            in_specs=[
                pl.BlockSpec((192, 128), lambda j, pos: (0, 0)),
                pl.BlockSpec((192, 256), lambda j, pos: (0, 2 * j + pos[0])),
                pl.BlockSpec((192, 256), lambda j, pos: (0, 2 * j + 1 - pos[0])),
                pl.BlockSpec((128, 64), lambda j, pos: (0, 0)),
            ],
            out_specs=[pl.BlockSpec((1, 128, 256), lambda j, pos: (j, 0, 0))] * 2,
        ),
        out_shape=[block, block],
        cost_estimate=pl.CostEstimate(flops=2 * 192 * 128 * 8192, bytes_accessed=5 << 20, transcendentals=0),
        name="local_grads",
    )(pos, hidden, out_grad, out_grad, e1)


def hidden_kernel(pos, og, own, oth, out, wide, total):
    c, x, zh = pos[0], pos[1], pos[3]
    step = pl.program_id(0)

    @pl.when(step == 0)
    def _():
        total[...] = jnp.zeros_like(total)

    acc = total[...]
    for kz in range(4):
        at = lax.rem(zh + kz, 4) * 512
        for side, (core, part) in enumerate(((c, own), (1 - c, oth))):
            slot = 2 * kz + side
            for kx in range(4):
                row = pl.multiple_of(lax.rem(x + kx, 4) * 32, 32)
                wide[slot, pl.ds(row, 32), :] = part[kx, 0, kz]
            cols = og[:, pl.ds(pl.multiple_of(at + core * 256, 256), 256)]
            acc += lax.dot_general(cols, wide[slot], (((1,), (1,)), ((), ())), preferred_element_type=jnp.float32)
    total[...] = acc

    @pl.when(step == 3)
    def _():
        out[...] = total[...].astype(jnp.bfloat16)


def hidden_grads(pos, out_grad, own, oth):
    part = pl.BlockSpec((4, 1, 4, 32, 256), lambda k, pos: (0, k, 0, 0, 0))
    return pl.pallas_call(
        hidden_kernel,
        grid_spec=pltpu.PrefetchScalarGridSpec(
            num_scalar_prefetch=1,
            grid=(4,),
            in_specs=[pl.BlockSpec((192, 2048), lambda k, pos: (0, lax.rem(pos[2] + k, 4))), part, part],
            out_specs=pl.BlockSpec((192, 128), lambda k, pos: (0, 0)),
            scratch_shapes=[pltpu.VMEM((8, 128, 256), jnp.bfloat16), pltpu.VMEM((192, 128), jnp.float32)],
        ),
        out_shape=jax.ShapeDtypeStruct((192, 128), jnp.bfloat16),
        cost_estimate=pl.CostEstimate(flops=2 * 192 * 128 * 8192, bytes_accessed=5 << 20, transcendentals=0),
        name="hidden_grads",
    )(pos, out_grad, own, oth)


def gather(value, axis):
    return jnp.stack([value] + [shifted(value, axis, k) for k in (1, 2, 3)])


def per_device(out_grad, hidden, weight, e1, e2):
    x, y, zh, c = (lax.axis_index(a) for a in ("x", "y", "zh", "c"))
    pos = jnp.stack([c, x, y, zh]).astype(jnp.int32)
    f32, bf16 = jnp.float32, jnp.bfloat16

    own, oth = local_grads(pos, hidden, out_grad, e1)
    got = shifted(oth, "c", 1)
    pair = (own.astype(f32) + got.astype(f32)).astype(bf16).reshape(4, 4, 128, 256)
    cols = lax.all_to_all(pair, "y", 0, 0, tiled=True)
    line = cols.astype(f32).sum(0).astype(bf16)
    group = lax.dynamic_index_in_dim(line, zh, 0, False).astype(f32)
    for k in (1, 2, 3):
        block = lax.dynamic_index_in_dim(line, lax.rem(zh + k, 4), 0, False)
        group = group + sent(block, "zh", k).astype(f32)
    limit = jnp.left_shift(1, e2 + 16).astype(f32) * (LIMIT * 2.0**-16)
    limit = jnp.repeat(limit, 128, axis=1)
    again = jnp.clip(group, -limit, limit).astype(bf16)
    rows = lax.all_to_all(again.reshape(SIZES["x"] * SIZES["zl"], -1, 256), OUTER, 0, 0, tiled=True)
    weight_grad = rows.astype(f32).sum(0)

    part = lax.dynamic_slice_in_dim(weight, x * 32, 32, 0)
    part = gather(part, "zh")
    part = gather(part, "y")
    part = gather(part, "x")
    hidden_grad = hidden_grads(pos, out_grad, part, shifted(part, "c", 1))
    return hidden_grad, weight_grad


def solution(mesh):
    fine = Mesh(mesh.devices.reshape(tuple(SIZES.values())), AXES)
    every, inner = P(AXES, None), ("y", "zh", "c")
    return jax.shard_map(
        per_device,
        mesh=fine,
        in_specs=(every, every, P(None, inner), every, P(OUTER, inner)),
        out_specs=(every, P(OUTER, inner)),
        check_vma=False,
    )
```

```python
import jax
import jax.numpy as jnp
from jax import lax
from jax.experimental import pallas as pl
from jax.experimental.pallas import tpu as pltpu
from jax.sharding import Mesh, PartitionSpec as P

SIZES = {"x": 4, "zl": 8, "y": 4, "zh": 4, "c": 2}
AXES = tuple(SIZES)
OUTER = ("x", "zl")
N_OUTER = 32
LIMIT = 448.0
F32, BF16 = jnp.float32, jnp.bfloat16


def limits(exponent):
    return jnp.left_shift(1, exponent + 16).astype(F32) * (LIMIT * 2.0**-16)


def grad_kernel(hid, og, exponent, out):
    bound = limits(exponent[...]).astype(BF16)
    acts = hid[...].T
    rows = lax.broadcasted_iota(jnp.int32, (16, 256), 0)
    lanes = lax.broadcasted_iota(jnp.int32, (16, 256), 1) // 128
    for block in range(8):
        pick = (rows == 2 * block + lanes).astype(BF16)
        limit = lax.dot_general(bound, pick, (((0,), (0,)), ((), ())), preferred_element_type=F32)
        local = jnp.dot(acts, og[:, 256 * block : 256 * (block + 1)], preferred_element_type=F32)
        out[block % 2, block // 2] = jnp.clip(local, -limit, limit).astype(BF16)


def local_grads(hidden, out_grad, exponent):
    return pl.pallas_call(
        grad_kernel,
        grid=(4,),
        in_specs=[
            pl.BlockSpec((192, 128), lambda y: (0, 0)),
            pl.BlockSpec((192, 2048), lambda y: (0, y)),
            pl.BlockSpec((16, 128), lambda y: (y, 0)),
        ],
        out_specs=pl.BlockSpec((2, 4, 128, 256), lambda y: (0, y, 0, 0)),
        out_shape=jax.ShapeDtypeStruct((2, 16, 128, 256), BF16),
        cost_estimate=pl.CostEstimate(flops=2 * 192 * 128 * 8192, bytes_accessed=5 << 20, transcendentals=0),
        name="local_grads",
    )(hidden, out_grad, exponent)


def hidden_kernel(core, og, own, oth, out, total):
    step, c = pl.program_id(0), core[0]

    @pl.when(step == 0)
    def _():
        total[...] = jnp.zeros_like(total)

    acc = total[...]
    for zh in range(4):
        for side, part in ((c, own), (1 - c, oth)):
            cols = og[:, pl.ds(pl.multiple_of(512 * zh + 256 * side, 256), 256)]
            rows = part[:, 0, zh].reshape(128, 256)
            acc += lax.dot_general(cols, rows, (((1,), (1,)), ((), ())), preferred_element_type=F32)
    total[...] = acc

    @pl.when(step == 3)
    def _():
        out[...] = acc.astype(BF16)


def hidden_grads(core, out_grad, own, oth):
    part = pl.BlockSpec((4, 1, 4, 32, 256), lambda y, core: (0, y, 0, 0, 0))
    return pl.pallas_call(
        hidden_kernel,
        grid_spec=pltpu.PrefetchScalarGridSpec(
            num_scalar_prefetch=1,
            grid=(4,),
            in_specs=[pl.BlockSpec((192, 2048), lambda y, core: (0, y)), part, part],
            out_specs=pl.BlockSpec((192, 128), lambda y, core: (0, 0)),
            scratch_shapes=[pltpu.VMEM((192, 128), F32)],
        ),
        out_shape=jax.ShapeDtypeStruct((192, 128), BF16),
        cost_estimate=pl.CostEstimate(flops=2 * 192 * 128 * 8192, bytes_accessed=5 << 20, transcendentals=0),
        name="hidden_grads",
    )(core, out_grad, own, oth)


def swap(value, axes):
    return lax.all_to_all(value, axes, 0, 0, tiled=True)


def after(value, *earlier):
    return lax.optimization_barrier((value, *earlier))[0]


def summed(parts):
    return parts.astype(F32).sum(0)


def per_device(out_grad, hidden, weight, e1, e2):
    x, c = lax.axis_index("x"), lax.axis_index("c")
    blocks = local_grads(hidden, out_grad, e1.T)
    pairs = summed(swap(blocks, "c")).astype(BF16)

    mine = after(lax.dynamic_slice_in_dim(weight, x * 32, 32, 0), blocks)
    quarter = swap(jnp.broadcast_to(mine, (4, 32, 256)), "zh")

    columns = swap(pairs.reshape(4, 4, 128, 256), "y")
    line = summed(columns).astype(BF16)
    group = summed(swap(line, "zh"))
    limit = jnp.repeat(limits(e2), 128, axis=1)
    again = jnp.clip(group, -limit, limit).astype(BF16)
    rows = swap(again.reshape(N_OUTER, -1, 256), OUTER)
    weight_grad = summed(rows)

    quarter = after(quarter, line)
    own = swap(jnp.broadcast_to(quarter, (16, 4, 32, 256)), ("x", "y")).reshape(4, 4, 4, 32, 256)
    oth = lax.ppermute(own, "c", [(0, 1), (1, 0)])
    hidden_grad = hidden_grads(c[None], out_grad, own, oth)
    return hidden_grad, weight_grad


def solution(mesh):
    fine = Mesh(mesh.devices.reshape(tuple(SIZES.values())), AXES)
    every, inner = P(AXES, None), ("y", "zh", "c")
    return jax.shard_map(
        per_device,
        mesh=fine,
        in_specs=(every, every, P(None, inner), every, P(OUTER, inner)),
        out_specs=(every, P(OUTER, inner)),
        check_vma=False,
    )
```

```python
import jax
import jax.numpy as jnp
from jax import lax
from jax.experimental import pallas as pl
from jax.experimental.pallas import tpu as pltpu
from jax.sharding import Mesh, PartitionSpec as P

SIZES = {"x": 4, "zl": 8, "y": 4, "zh": 4, "c": 2}
AXES = tuple(SIZES)
OUTER = ("x", "zl")
N_OUTER = 32
LIMIT = 448.0
F32, BF16 = jnp.float32, jnp.bfloat16


def limits(exponent):
    return jnp.left_shift(1, exponent + 16).astype(F32) * (LIMIT * 2.0**-16)


def grad_kernel(core, hid, og0, og1, og2, og3, exponent, out):
    bound = limits(exponent[...]).astype(BF16)
    acts = hid[...].T
    rows = lax.broadcasted_iota(jnp.int32, (16, 256), 0)
    lanes = lax.broadcasted_iota(jnp.int32, (16, 256), 1) // 128 + 2 * core[0]
    for zh, og in enumerate((og0, og1, og2, og3)):
        pick = (rows == 4 * zh + lanes).astype(BF16)
        limit = lax.dot_general(bound, pick, (((0,), (0,)), ((), ())), preferred_element_type=F32)
        local = jnp.dot(acts, og[...], preferred_element_type=F32)
        out[zh] = jnp.clip(local, -limit, limit).astype(BF16)


def local_grads(core, hidden, out_grad, exponent):
    columns = [pl.BlockSpec((192, 256), lambda y, core, k=2 * zh: (0, 8 * y + k + core[0])) for zh in range(4)]
    return pl.pallas_call(
        grad_kernel,
        grid_spec=pltpu.PrefetchScalarGridSpec(
            num_scalar_prefetch=1,
            grid=(4,),
            in_specs=[
                pl.BlockSpec((192, 128), lambda y, core: (0, 0)),
                *columns,
                pl.BlockSpec((16, 128), lambda y, core: (y, 0)),
            ],
            out_specs=pl.BlockSpec((4, 128, 256), lambda y, core: (y, 0, 0)),
        ),
        out_shape=jax.ShapeDtypeStruct((16, 128, 256), BF16),
        cost_estimate=pl.CostEstimate(flops=192 * 128 * 8192, bytes_accessed=5 << 19, transcendentals=0),
        name="local_grads",
    )(core, hidden, out_grad, out_grad, out_grad, out_grad, exponent)


def hidden_kernel(pos, og, own, oth, out, wide, total):
    c, x, zh = pos[0], pos[1], pos[3]
    step = pl.program_id(0)

    @pl.when(step == 0)
    def _():
        total[...] = jnp.zeros_like(total)

    acc = total[...]
    for kz in range(4):
        at = lax.rem(zh + kz, 4) * 512
        for side, (core, part) in enumerate(((c, own), (1 - c, oth))):
            slot = 2 * kz + side
            for kx in range(4):
                row = pl.multiple_of(lax.rem(x + kx, 4) * 32, 32)
                wide[slot, pl.ds(row, 32), :] = part[kx, 0, kz]
            cols = og[:, pl.ds(pl.multiple_of(at + core * 256, 256), 256)]
            acc += lax.dot_general(cols, wide[slot], (((1,), (1,)), ((), ())), preferred_element_type=F32)
    total[...] = acc

    @pl.when(step == 3)
    def _():
        out[...] = acc.astype(BF16)


def hidden_grads(pos, out_grad, own, oth):
    part = pl.BlockSpec((4, 1, 4, 32, 256), lambda k, pos: (0, k, 0, 0, 0))
    return pl.pallas_call(
        hidden_kernel,
        grid_spec=pltpu.PrefetchScalarGridSpec(
            num_scalar_prefetch=1,
            grid=(4,),
            in_specs=[pl.BlockSpec((192, 2048), lambda k, pos: (0, lax.rem(pos[2] + k, 4))), part, part],
            out_specs=pl.BlockSpec((192, 128), lambda k, pos: (0, 0)),
            scratch_shapes=[pltpu.VMEM((8, 128, 256), BF16), pltpu.VMEM((192, 128), F32)],
        ),
        out_shape=jax.ShapeDtypeStruct((192, 128), BF16),
        cost_estimate=pl.CostEstimate(flops=2 * 192 * 128 * 8192, bytes_accessed=5 << 20, transcendentals=0),
        name="hidden_grads",
    )(pos, out_grad, own, oth)


def shifted(value, axis, k):
    n = SIZES[axis]
    return lax.ppermute(value, axis, [(i, (i - k) % n) for i in range(n)])


def gather(value, axis):
    return jnp.stack([value] + [shifted(value, axis, k) for k in (1, 2, 3)])


def swap(value, axes):
    return lax.all_to_all(value, axes, 0, 0, tiled=True)


def after(value, *earlier):
    return lax.optimization_barrier((value, *earlier))[0]


def summed(parts):
    return parts.astype(F32).sum(0)


def per_device(out_grad, hidden, weight, e1, e2):
    x, y, zh, c = (lax.axis_index(a) for a in ("x", "y", "zh", "c"))
    oth = local_grads(1 - c[None], hidden, out_grad, e1.T)
    got = shifted(oth, "c", 1)
    own = local_grads(after(c, oth)[None], hidden, out_grad, e1.T)
    pairs = (own.astype(F32) + got.astype(F32)).astype(BF16)
    columns = swap(pairs.reshape(4, 4, 128, 256), "y")

    part = after(lax.dynamic_slice_in_dim(weight, x * 32, 32, 0), pairs)
    part = gather(part, "zh")

    line = summed(columns).astype(BF16)
    group = summed(swap(line, "zh"))
    limit = jnp.repeat(limits(e2), 128, axis=1)
    again = jnp.clip(group, -limit, limit).astype(BF16)
    rows = swap(again.reshape(N_OUTER, -1, 256), OUTER)
    weight_grad = summed(rows)

    part = gather(after(part, line), "y")
    part = gather(part, "x")
    pos = jnp.stack([c, x, y, zh])
    hidden_grad = hidden_grads(pos, out_grad, part, shifted(part, "c", 1))
    return hidden_grad, weight_grad


def solution(mesh):
    fine = Mesh(mesh.devices.reshape(tuple(SIZES.values())), AXES)
    every, inner = P(AXES, None), ("y", "zh", "c")
    return jax.shard_map(
        per_device,
        mesh=fine,
        in_specs=(every, every, P(None, inner), every, P(OUTER, inner)),
        out_specs=(every, P(OUTER, inner)),
        check_vma=False,
    )
```

```python
import jax
import jax.numpy as jnp
from jax import lax
from jax.experimental import pallas as pl
from jax.experimental.pallas import tpu as pltpu
from jax.sharding import Mesh, PartitionSpec as P

SIZES = {"x": 4, "zl": 8, "y": 4, "zh": 4, "c": 2}
AXES = tuple(SIZES)
OUTER = ("x", "zl")
N_OUTER = 32
LIMIT = 448.0
VMEM = 8 << 20
F32, BF16 = jnp.float32, jnp.bfloat16


def limits(exponent):
    return jnp.left_shift(1, exponent + 16).astype(F32) * (LIMIT * 2.0**-16)


def grad_kernel(core, hid, og, exponent, own, oth, acts):
    c = core[0]

    @pl.when(pl.program_id(0) == 0)
    def _():
        acts[...] = hid[...].T

    bound = limits(exponent[...])
    other = pltpu.roll(bound, 14, 0)
    for side, out in ((c, own), (1 - c, oth)):
        mine = jnp.where(side == 0, bound, other).T
        for zh in range(4):
            cols = og[:, pl.ds(pl.multiple_of(512 * zh + 256 * side, 256), 256)]
            local = jnp.dot(acts[...], cols, preferred_element_type=F32)
            for half in range(2):
                most = mine[:, 4 * zh + half : 4 * zh + half + 1]
                lanes = slice(128 * half, 128 * half + 128)
                out[zh, :, lanes] = jnp.clip(local[:, lanes], -most, most).astype(BF16)


def local_grads(core, hidden, out_grad, exponent):
    block = jax.ShapeDtypeStruct((16, 128, 256), BF16)
    return pl.pallas_call(
        grad_kernel,
        grid_spec=pltpu.PrefetchScalarGridSpec(
            num_scalar_prefetch=1,
            grid=(4,),
            in_specs=[
                pl.BlockSpec((192, 128), lambda y, core: (0, 0)),
                pl.BlockSpec((192, 2048), lambda y, core: (0, y)),
                pl.BlockSpec((16, 128), lambda y, core: (y, 0)),
            ],
            out_specs=[pl.BlockSpec((4, 128, 256), lambda y, core: (y, 0, 0))] * 2,
            scratch_shapes=[pltpu.VMEM((128, 192), BF16)],
        ),
        out_shape=[block, block],
        compiler_params=pltpu.CompilerParams(vmem_limit_bytes=VMEM),
        cost_estimate=pl.CostEstimate(flops=1 << 20, bytes_accessed=1 << 16, transcendentals=0),
        name="local_grads",
    )(core, hidden, out_grad, exponent)


def join_kernel(own, got, quarter, out):
    for zh in range(4):
        out[0, 128 * zh : 128 * (zh + 1)] = (own[zh].astype(F32) + got[zh].astype(F32)).astype(BF16)
    out[0, 512:] = quarter[...].reshape(128, 256)


def joined(own, got, quarter):
    block = pl.BlockSpec((4, 128, 256), lambda y: (y, 0, 0))
    return pl.pallas_call(
        join_kernel,
        grid=(4,),
        in_specs=[block, block, pl.BlockSpec((4, 32, 256), lambda y: (0, 0, 0))],
        out_specs=pl.BlockSpec((1, 640, 256), lambda y: (y, 0, 0)),
        out_shape=jax.ShapeDtypeStruct((4, 640, 256), BF16),
        compiler_params=pltpu.CompilerParams(vmem_limit_bytes=VMEM),
        cost_estimate=pl.CostEstimate(flops=1 << 20, bytes_accessed=13 << 18, transcendentals=0),
        name="joined",
    )(own, got, quarter)


def hidden_kernel(pos, og, own, oth, out, total):
    c, x = pos[0], pos[1]
    step = pl.program_id(0)

    @pl.when(step == 0)
    def _():
        total[...] = jnp.zeros_like(total)

    acc = total[...]
    for zh in range(4):
        for core, part in ((c, own), (1 - c, oth)):
            rows = part[:, 0, 32 * zh : 32 * (zh + 1)].reshape(128, 256)
            cols = og[:, pl.ds(pl.multiple_of(512 * zh + core * 256, 256), 256)]
            acc += lax.dot_general(cols, rows, (((1,), (1,)), ((), ())), preferred_element_type=F32)
    total[...] = acc

    @pl.when(step == 3)
    def _():
        out[...] = pltpu.roll(acc, 32 * x, 1).astype(BF16)


def hidden_grads(pos, out_grad, own, oth):
    part = pl.BlockSpec((4, 1, 128, 256), lambda y, pos: (0, y, 0, 0))
    return pl.pallas_call(
        hidden_kernel,
        grid_spec=pltpu.PrefetchScalarGridSpec(
            num_scalar_prefetch=1,
            grid=(4,),
            in_specs=[pl.BlockSpec((192, 2048), lambda y, pos: (0, y)), part, part],
            out_specs=pl.BlockSpec((192, 128), lambda y, pos: (0, 0)),
            scratch_shapes=[pltpu.VMEM((192, 128), F32)],
        ),
        out_shape=jax.ShapeDtypeStruct((192, 128), BF16),
        compiler_params=pltpu.CompilerParams(vmem_limit_bytes=VMEM),
        cost_estimate=pl.CostEstimate(flops=2 * 192 * 128 * 8192, bytes_accessed=5 << 20, transcendentals=0),
        name="hidden_grads",
    )(pos, out_grad, own, oth)


def shifted(value, axis, k):
    n = SIZES[axis]
    return lax.ppermute(value, axis, [(i, (i - k) % n) for i in range(n)])


def gather(value, axis):
    return jnp.stack([value] + [shifted(value, axis, k) for k in (1, 2, 3)])


def swap(value, axes):
    return lax.all_to_all(value, axes, 0, 0, tiled=True)


def after(value, *earlier):
    return lax.optimization_barrier((value, *earlier))[0]


def summed(parts):
    return parts.astype(F32).sum(0)


def per_device(out_grad, hidden, weight, e1, e2):
    x, c = lax.axis_index("x"), lax.axis_index("c")
    mine = lax.dynamic_slice_in_dim(weight, x * 32, 32, 0)
    quarter = swap(jnp.broadcast_to(mine, (4, 32, 256)), "zh")

    own, oth = local_grads(c[None], hidden, out_grad, e1.T)
    got = shifted(oth, "c", 1)
    columns = swap(joined(own, got, quarter), "y")

    line = summed(columns[:, :512].reshape(4, 4, 128, 256)).astype(BF16)
    group = summed(swap(line, "zh"))
    limit = jnp.repeat(limits(e2), 128, axis=1)
    again = jnp.clip(group, -limit, limit).astype(BF16)
    rows = swap(again.reshape(N_OUTER, -1, 256), OUTER)
    weight_grad = summed(rows)

    part = gather(after(columns[:, 512:], line), "x")
    hidden_grad = hidden_grads(jnp.stack([c, x]), out_grad, part, shifted(part, "c", 1))
    return hidden_grad, weight_grad


def solution(mesh):
    fine = Mesh(mesh.devices.reshape(tuple(SIZES.values())), AXES)
    every, inner = P(AXES, None), ("y", "zh", "c")
    return jax.shard_map(
        per_device,
        mesh=fine,
        in_specs=(every, every, P(None, inner), every, P(OUTER, inner)),
        out_specs=(every, P(OUTER, inner)),
        check_vma=False,
    )
```

```python
import jax
import jax.numpy as jnp
from jax import lax
from jax.experimental import pallas as pl
from jax.experimental.pallas import tpu as pltpu
from jax.sharding import Mesh, PartitionSpec as P

SIZES = {"x": 4, "zl": 8, "y": 4, "zh": 4, "c": 2}
AXES = tuple(SIZES)
OUTER = ("x", "zl")
N_OUTER = 32
LIMIT = 448.0
VMEM = 8 << 20
ORDER = (0, 1, 3, 2)
F32, BF16 = jnp.float32, jnp.bfloat16


def limits(exponent):
    return jnp.left_shift(1, exponent + 16).astype(F32) * (LIMIT * 2.0**-16)


def grad_kernel(core, hid, og, exponent, own, oth, acts):
    c = core[0]

    @pl.when(pl.program_id(0) == 0)
    def _():
        acts[...] = hid[...].T

    bound = limits(exponent[...])
    other = pltpu.roll(bound, 14, 0)
    for side, out in ((c, own), (1 - c, oth)):
        mine = jnp.where(side == 0, bound, other).T
        for zh in range(4):
            cols = og[:, pl.ds(pl.multiple_of(512 * zh + 256 * side, 256), 256)]
            local = jnp.dot(acts[...], cols, preferred_element_type=F32)
            for half in range(2):
                most = mine[:, 4 * zh + half : 4 * zh + half + 1]
                lanes = slice(128 * half, 128 * half + 128)
                out[zh, :, lanes] = jnp.clip(local[:, lanes], -most, most).astype(BF16)


def local_grads(core, hidden, out_grad, exponent):
    block = jax.ShapeDtypeStruct((16, 128, 256), BF16)
    return pl.pallas_call(
        grad_kernel,
        grid_spec=pltpu.PrefetchScalarGridSpec(
            num_scalar_prefetch=1,
            grid=(4,),
            in_specs=[
                pl.BlockSpec((192, 128), lambda y, core: (0, 0)),
                pl.BlockSpec((192, 2048), lambda y, core: (0, y)),
                pl.BlockSpec((16, 128), lambda y, core: (y, 0)),
            ],
            out_specs=[pl.BlockSpec((4, 128, 256), lambda y, core: (y, 0, 0))] * 2,
            scratch_shapes=[pltpu.VMEM((128, 192), BF16)],
        ),
        out_shape=[block, block],
        compiler_params=pltpu.CompilerParams(vmem_limit_bytes=VMEM),
        cost_estimate=pl.CostEstimate(flops=1 << 20, bytes_accessed=1 << 16, transcendentals=0),
        name="local_grads",
    )(core, hidden, out_grad, exponent)


def pair_kernel(own, got, out):
    out[...] = (own[...].astype(F32) + got[...].astype(F32)).astype(BF16)


def paired(own, got):
    block = pl.BlockSpec((4, 128, 256), lambda y: (y, 0, 0))
    return pl.pallas_call(
        pair_kernel,
        grid=(4,),
        in_specs=[block, block],
        out_specs=block,
        out_shape=jax.ShapeDtypeStruct((16, 128, 256), BF16),
        compiler_params=pltpu.CompilerParams(vmem_limit_bytes=VMEM),
        cost_estimate=pl.CostEstimate(flops=1 << 20, bytes_accessed=3 << 20, transcendentals=0),
        name="paired",
    )(own, got).reshape(4, 4, 128, 256)


def hidden_kernel(pos, og, own, oth, out, total):
    c, x, zh = pos[0], pos[1], pos[3]
    step = pl.program_id(0)

    @pl.when(step == 0)
    def _():
        total[...] = jnp.zeros_like(total)

    acc = total[...]
    for k, bits in enumerate(ORDER):
        for core, part in ((c, own), (1 - c, oth)):
            rows = part[:, 0, k].reshape(128, 256)
            at = pl.multiple_of(512 * jnp.bitwise_xor(zh, bits) + core * 256, 256)
            acc += lax.dot_general(og[:, pl.ds(at, 256)], rows, (((1,), (1,)), ((), ())), preferred_element_type=F32)
    total[...] = acc

    @pl.when(step == 3)
    def _():
        out[...] = pltpu.roll(acc, 32 * x, 1).astype(BF16)


def hidden_grads(pos, out_grad, own, oth):
    part = pl.BlockSpec((4, 1, 4, 32, 256), lambda k, pos: (0, k, 0, 0, 0))
    return pl.pallas_call(
        hidden_kernel,
        grid_spec=pltpu.PrefetchScalarGridSpec(
            num_scalar_prefetch=1,
            grid=(4,),
            in_specs=[pl.BlockSpec((192, 2048), lambda k, pos: (0, lax.rem(pos[2] + k, 4))), part, part],
            out_specs=pl.BlockSpec((192, 128), lambda k, pos: (0, 0)),
            scratch_shapes=[pltpu.VMEM((192, 128), F32)],
        ),
        out_shape=jax.ShapeDtypeStruct((192, 128), BF16),
        compiler_params=pltpu.CompilerParams(vmem_limit_bytes=VMEM),
        cost_estimate=pl.CostEstimate(flops=2 * 192 * 128 * 8192, bytes_accessed=5 << 20, transcendentals=0),
        name="hidden_grads",
    )(pos, out_grad, own, oth)


def exchanged(value, axis, bits):
    return lax.ppermute(value, axis, [(i, i ^ bits) for i in range(SIZES[axis])])


def shifted(value, axis, k):
    n = SIZES[axis]
    return lax.ppermute(value, axis, [(i, (i - k) % n) for i in range(n)])


def gather(value, axis):
    return jnp.stack([value] + [shifted(value, axis, k) for k in (1, 2, 3)])


def swap(value, axes):
    return lax.all_to_all(value, axes, 0, 0, tiled=True)


def after(value, *earlier):
    return lax.optimization_barrier((value, *earlier))[0]


def summed(parts):
    return parts.astype(F32).sum(0)


def per_device(out_grad, hidden, weight, e1, e2):
    x, y, zh, c = (lax.axis_index(a) for a in ("x", "y", "zh", "c"))
    mine = lax.dynamic_slice_in_dim(weight, x * 32, 32, 0)
    near = exchanged(mine, "zh", 1)

    own, oth = local_grads(c[None], hidden, out_grad, e1.T)
    got = shifted(after(oth, near), "c", 1)
    pairs = paired(own, got)
    columns = swap(pairs, "y")
    line = summed(columns).astype(BF16)

    two = jnp.stack([mine, after(near, pairs)])
    quarter = jnp.concatenate([two, exchanged(two, "zh", 3)])

    group = summed(swap(after(line, quarter), "zh"))
    limit = jnp.repeat(limits(e2), 128, axis=1)
    again = jnp.clip(group, -limit, limit).astype(BF16)
    rows = swap(again.reshape(N_OUTER, -1, 256), OUTER)
    weight_grad = summed(rows)

    part = gather(gather(after(quarter, line), "y"), "x")
    pos = jnp.stack([c, x, y, zh])
    hidden_grad = hidden_grads(pos, out_grad, part, shifted(part, "c", 1))
    return hidden_grad, weight_grad


def solution(mesh):
    fine = Mesh(mesh.devices.reshape(tuple(SIZES.values())), AXES)
    every, inner = P(AXES, None), ("y", "zh", "c")
    return jax.shard_map(
        per_device,
        mesh=fine,
        in_specs=(every, every, P(None, inner), every, P(OUTER, inner)),
        out_specs=(every, P(OUTER, inner)),
        check_vma=False,
    )
```

```python
import jax
import jax.numpy as jnp
from jax import lax
from jax.experimental import pallas as pl
from jax.experimental.pallas import tpu as pltpu
from jax.sharding import Mesh, PartitionSpec as P

SIZES = {"x": 4, "zl": 8, "y": 4, "zh": 4, "c": 2}
AXES = tuple(SIZES)
OUTER = ("x", "zl")
N_OUTER = 32
LIMIT = 448.0
VMEM = 8 << 20
ORDER = (0, 1, 3, 2)
F32, BF16 = jnp.float32, jnp.bfloat16


def limits(exponent):
    return jnp.left_shift(1, exponent + 16).astype(F32) * (LIMIT * 2.0**-16)


def grad_kernel(core, hid, og, exponent, own, oth, acts):
    c = core[0]

    @pl.when(pl.program_id(0) == 0)
    def _():
        acts[...] = hid[...].T

    bound = limits(exponent[...])
    other = pltpu.roll(bound, 14, 0)
    for side, out in ((c, own), (1 - c, oth)):
        mine = jnp.where(side == 0, bound, other).T
        for zh in range(4):
            cols = og[:, pl.ds(pl.multiple_of(512 * zh + 256 * side, 256), 256)]
            local = jnp.dot(acts[...], cols, preferred_element_type=F32)
            for half in range(2):
                most = mine[:, 4 * zh + half : 4 * zh + half + 1]
                lanes = slice(128 * half, 128 * half + 128)
                out[zh, :, lanes] = jnp.clip(local[:, lanes], -most, most).astype(BF16)


def local_grads(core, hidden, out_grad, exponent):
    block = jax.ShapeDtypeStruct((16, 128, 256), BF16)
    return pl.pallas_call(
        grad_kernel,
        grid_spec=pltpu.PrefetchScalarGridSpec(
            num_scalar_prefetch=1,
            grid=(4,),
            in_specs=[
                pl.BlockSpec((192, 128), lambda y, core: (0, 0)),
                pl.BlockSpec((192, 2048), lambda y, core: (0, y)),
                pl.BlockSpec((16, 128), lambda y, core: (y, 0)),
            ],
            out_specs=[pl.BlockSpec((4, 128, 256), lambda y, core: (y, 0, 0))] * 2,
            scratch_shapes=[pltpu.VMEM((128, 192), BF16)],
        ),
        out_shape=[block, block],
        compiler_params=pltpu.CompilerParams(vmem_limit_bytes=VMEM),
        cost_estimate=pl.CostEstimate(flops=1 << 20, bytes_accessed=1 << 16, transcendentals=0),
        name="local_grads",
    )(core, hidden, out_grad, exponent)


def pair_kernel(own, got, out):
    out[...] = (own[...].astype(F32) + got[...].astype(F32)).astype(BF16)


def paired(own, got):
    block = pl.BlockSpec((4, 128, 256), lambda y: (y, 0, 0))
    return pl.pallas_call(
        pair_kernel,
        grid=(4,),
        in_specs=[block, block],
        out_specs=block,
        out_shape=jax.ShapeDtypeStruct((16, 128, 256), BF16),
        compiler_params=pltpu.CompilerParams(vmem_limit_bytes=VMEM),
        cost_estimate=pl.CostEstimate(flops=1 << 20, bytes_accessed=3 << 20, transcendentals=0),
        name="paired",
    )(own, got).reshape(4, 4, 128, 256)


def hidden_kernel(pos, og, own, oth, out, total):
    c, x, zh = pos[0], pos[1], pos[3]
    step = pl.program_id(0)

    @pl.when(step == 0)
    def _():
        total[...] = jnp.zeros_like(total)

    acc = total[...]
    for k, bits in enumerate(ORDER):
        for core, part in ((c, own), (1 - c, oth)):
            rows = part[0, :, k].reshape(128, 256)
            at = pl.multiple_of(512 * jnp.bitwise_xor(zh, bits) + core * 256, 256)
            acc += lax.dot_general(og[:, pl.ds(at, 256)], rows, (((1,), (1,)), ((), ())), preferred_element_type=F32)
    total[...] = acc

    @pl.when(step == 3)
    def _():
        out[...] = pltpu.roll(acc, 32 * x, 1).astype(BF16)


def hidden_grads(pos, out_grad, own, oth):
    part = pl.BlockSpec((1, 4, 4, 32, 256), lambda k, pos: (k, 0, 0, 0, 0))
    return pl.pallas_call(
        hidden_kernel,
        grid_spec=pltpu.PrefetchScalarGridSpec(
            num_scalar_prefetch=1,
            grid=(4,),
            in_specs=[pl.BlockSpec((192, 2048), lambda k, pos: (0, lax.rem(pos[2] + k, 4))), part, part],
            out_specs=pl.BlockSpec((192, 128), lambda k, pos: (0, 0)),
            scratch_shapes=[pltpu.VMEM((192, 128), F32)],
        ),
        out_shape=jax.ShapeDtypeStruct((192, 128), BF16),
        compiler_params=pltpu.CompilerParams(vmem_limit_bytes=VMEM),
        cost_estimate=pl.CostEstimate(flops=2 * 192 * 128 * 8192, bytes_accessed=5 << 20, transcendentals=0),
        name="hidden_grads",
    )(pos, out_grad, own, oth)


def line_kernel(parts, out):
    out[0] = parts[:, 0].astype(F32).sum(0).astype(BF16)


def lined(parts):
    return pl.pallas_call(
        line_kernel,
        grid=(4,),
        in_specs=[pl.BlockSpec((4, 1, 128, 256), lambda zh: (0, zh, 0, 0))],
        out_specs=pl.BlockSpec((1, 128, 256), lambda zh: (zh, 0, 0)),
        out_shape=jax.ShapeDtypeStruct((4, 128, 256), BF16),
        compiler_params=pltpu.CompilerParams(vmem_limit_bytes=VMEM),
        cost_estimate=pl.CostEstimate(flops=1 << 19, bytes_accessed=5 << 18, transcendentals=0),
        name="lined",
    )(parts)


def again_kernel(parts, exponent, out):
    bound = limits(exponent[...]).T
    for half in range(2):
        lanes = slice(128 * half, 128 * half + 128)
        group = parts[:, :, lanes].astype(F32).sum(0)
        most = bound[:, half : half + 1]
        out[:, lanes] = jnp.clip(group, -most, most).astype(BF16)


def requantized(parts, exponent):
    return pl.pallas_call(
        again_kernel,
        out_shape=jax.ShapeDtypeStruct((128, 256), BF16),
        compiler_params=pltpu.CompilerParams(vmem_limit_bytes=VMEM),
        cost_estimate=pl.CostEstimate(flops=1 << 17, bytes_accessed=5 << 16, transcendentals=0),
        name="requantized",
    )(parts, exponent)


def exchanged(value, axis, bits):
    return lax.ppermute(value, axis, [(i, i ^ bits) for i in range(SIZES[axis])])


def shifted(value, axis, k):
    n = SIZES[axis]
    return lax.ppermute(value, axis, [(i, (i - k) % n) for i in range(n)])


def pieces(value, axis):
    return [value] + [shifted(value, axis, k) for k in (1, 2, 3)]


def swap(value, axes):
    return lax.all_to_all(value, axes, 0, 0, tiled=True)


def after(value, *earlier):
    return lax.optimization_barrier((value, *earlier))[0]


def summed(parts):
    return parts.astype(F32).sum(0)


def per_device(out_grad, hidden, weight, e1, e2):
    x, y, zh, c = (lax.axis_index(a) for a in ("x", "y", "zh", "c"))
    mine = lax.dynamic_slice_in_dim(weight, x * 32, 32, 0)
    near = exchanged(mine, "zh", 1)

    own, oth = local_grads(c[None], hidden, out_grad, e1.T)
    got = shifted(after(oth, near), "c", 1)
    pairs = paired(own, got)
    columns = swap(pairs, "y")
    two = jnp.stack([mine, after(near, pairs)])
    quarter = jnp.concatenate([two, exchanged(two, "zh", 3)])

    line = lined(columns)
    again = requantized(swap(after(line, quarter), "zh"), e2.T)
    rows = swap(again.reshape(N_OUTER, -1, 256), OUTER)

    part = jnp.stack(pieces(after(quarter, line), "x"))
    part = jnp.stack([after(piece, again) for piece in pieces(part, "y")])
    pos = jnp.stack([c, x, y, zh])
    hidden_grad = hidden_grads(pos, out_grad, part, shifted(part, "c", 1))
    return hidden_grad, summed(after(rows, hidden_grad))


def solution(mesh):
    fine = Mesh(mesh.devices.reshape(tuple(SIZES.values())), AXES)
    every, inner = P(AXES, None), ("y", "zh", "c")
    return jax.shard_map(
        per_device,
        mesh=fine,
        in_specs=(every, every, P(None, inner), every, P(OUTER, inner)),
        out_specs=(every, P(OUTER, inner)),
        check_vma=False,
    )
```

```python
import jax
import jax.numpy as jnp
from jax import lax
from jax.experimental import pallas as pl
from jax.experimental.pallas import tpu as pltpu
from jax.sharding import Mesh, PartitionSpec as P

SIZES = {"x": 4, "zl": 8, "y": 4, "zh": 4, "c": 2}
AXES = tuple(SIZES)
OUTER = ("x", "zl")
N_OUTER = 32
LIMIT = 448.0
VMEM = 3 << 20
VMEM_LOCAL, VMEM_HIDDEN = 64_980_000, 64_500_000
ORDER = (0, 1, 3, 2)
F32, BF16 = jnp.float32, jnp.bfloat16


def limits(exponent):
    return jnp.left_shift(1, exponent + 16).astype(F32) * (LIMIT * 2.0**-16)


def grad_kernel(core, hid, og, exponent, own, oth, acts):
    c = core[0]

    @pl.when(pl.program_id(0) == 0)
    def _():
        acts[...] = hid[...].T

    bound = limits(exponent[...])
    other = pltpu.roll(bound, 14, 0)
    for side, out in ((c, own), (1 - c, oth)):
        mine = jnp.where(side == 0, bound, other).T
        for zh in range(4):
            cols = og[:, pl.ds(pl.multiple_of(512 * zh + 256 * side, 256), 256)]
            local = jnp.dot(acts[...], cols, preferred_element_type=F32)
            for half in range(2):
                most = mine[:, 4 * zh + half : 4 * zh + half + 1]
                lanes = slice(128 * half, 128 * half + 128)
                out[zh, :, lanes] = jnp.clip(local[:, lanes], -most, most).astype(BF16)


def local_grads(core, hidden, out_grad, exponent):
    block = jax.ShapeDtypeStruct((16, 128, 256), BF16)
    return pl.pallas_call(
        grad_kernel,
        grid_spec=pltpu.PrefetchScalarGridSpec(
            num_scalar_prefetch=1,
            grid=(4,),
            in_specs=[
                pl.BlockSpec((192, 128), lambda y, core: (0, 0)),
                pl.BlockSpec((192, 2048), lambda y, core: (0, y)),
                pl.BlockSpec((16, 128), lambda y, core: (y, 0)),
            ],
            out_specs=[pl.BlockSpec((4, 128, 256), lambda y, core: (y, 0, 0))] * 2,
            scratch_shapes=[pltpu.VMEM((128, 192), BF16)],
        ),
        out_shape=[block, block],
        compiler_params=pltpu.CompilerParams(vmem_limit_bytes=VMEM_LOCAL),
        cost_estimate=pl.CostEstimate(flops=1 << 20, bytes_accessed=1 << 16, transcendentals=0),
        name="local_grads",
    )(core, hidden, out_grad, exponent)


def pair_kernel(own, got, out):
    out[...] = (own[...].astype(F32) + got[...].astype(F32)).astype(BF16)


def paired(own, got):
    block = pl.BlockSpec((4, 128, 256), lambda y: (y, 0, 0))
    return pl.pallas_call(
        pair_kernel,
        grid=(4,),
        in_specs=[block, block],
        out_specs=block,
        out_shape=jax.ShapeDtypeStruct((16, 128, 256), BF16),
        compiler_params=pltpu.CompilerParams(vmem_limit_bytes=VMEM),
        cost_estimate=pl.CostEstimate(flops=1 << 20, bytes_accessed=3 << 20, transcendentals=0),
        name="paired",
    )(own, got).reshape(4, 4, 128, 256)


def hidden_kernel(pos, og, own, oth, out, total):
    c, x, zh = pos[0], pos[1], pos[3]
    step = pl.program_id(0)

    @pl.when(step == 0)
    def _():
        total[...] = jnp.zeros_like(total)

    acc = total[...]
    for k, bits in enumerate(ORDER):
        for core, part in ((c, own), (1 - c, oth)):
            rows = part[0, :, k].reshape(128, 256)
            at = pl.multiple_of(512 * jnp.bitwise_xor(zh, bits) + core * 256, 256)
            acc += lax.dot_general(og[:, pl.ds(at, 256)], rows, (((1,), (1,)), ((), ())), preferred_element_type=F32)
    total[...] = acc

    @pl.when(step == 3)
    def _():
        out[...] = pltpu.roll(acc, 32 * x, 1).astype(BF16)


def hidden_grads(pos, out_grad, own, oth):
    part = pl.BlockSpec((1, 4, 4, 32, 256), lambda k, pos: (k, 0, 0, 0, 0))
    return pl.pallas_call(
        hidden_kernel,
        grid_spec=pltpu.PrefetchScalarGridSpec(
            num_scalar_prefetch=1,
            grid=(4,),
            in_specs=[pl.BlockSpec((192, 2048), lambda k, pos: (0, lax.rem(pos[2] + k, 4))), part, part],
            out_specs=pl.BlockSpec((192, 128), lambda k, pos: (0, 0)),
            scratch_shapes=[pltpu.VMEM((192, 128), F32)],
        ),
        out_shape=jax.ShapeDtypeStruct((192, 128), BF16),
        compiler_params=pltpu.CompilerParams(vmem_limit_bytes=VMEM_HIDDEN),
        cost_estimate=pl.CostEstimate(flops=2 * 192 * 128 * 8192, bytes_accessed=5 << 20, transcendentals=0),
        name="hidden_grads",
    )(pos, out_grad, own, oth)


def line_kernel(parts, out):
    out[0] = parts[:, 0].astype(F32).sum(0).astype(BF16)


def lined(parts):
    return pl.pallas_call(
        line_kernel,
        grid=(4,),
        in_specs=[pl.BlockSpec((4, 1, 128, 256), lambda zh: (0, zh, 0, 0))],
        out_specs=pl.BlockSpec((1, 128, 256), lambda zh: (zh, 0, 0)),
        out_shape=jax.ShapeDtypeStruct((4, 128, 256), BF16),
        compiler_params=pltpu.CompilerParams(vmem_limit_bytes=VMEM),
        cost_estimate=pl.CostEstimate(flops=1 << 19, bytes_accessed=5 << 18, transcendentals=0),
        name="lined",
    )(parts)


def again_kernel(parts, exponent, out):
    bound = limits(exponent[...]).T
    for half in range(2):
        lanes = slice(128 * half, 128 * half + 128)
        group = parts[:, :, lanes].astype(F32).sum(0)
        most = bound[:, half : half + 1]
        out[:, lanes] = jnp.clip(group, -most, most).astype(BF16)


def requantized(parts, exponent):
    return pl.pallas_call(
        again_kernel,
        out_shape=jax.ShapeDtypeStruct((128, 256), BF16),
        compiler_params=pltpu.CompilerParams(vmem_limit_bytes=VMEM),
        cost_estimate=pl.CostEstimate(flops=1 << 17, bytes_accessed=5 << 16, transcendentals=0),
        name="requantized",
    )(parts, exponent)


def exchanged(value, axis, bits):
    return lax.ppermute(value, axis, [(i, i ^ bits) for i in range(SIZES[axis])])


def shifted(value, axis, k):
    n = SIZES[axis]
    return lax.ppermute(value, axis, [(i, (i - k) % n) for i in range(n)])


def pieces(value, axis):
    return [value] + [shifted(value, axis, k) for k in (1, 2, 3)]


def swap(value, axes):
    return lax.all_to_all(value, axes, 0, 0, tiled=True)


def after(value, *earlier):
    return lax.optimization_barrier((value, *earlier))[0]


def summed(parts):
    return parts.astype(F32).sum(0)


def per_device(out_grad, hidden, weight, e1, e2):
    x, y, zh, c = (lax.axis_index(a) for a in ("x", "y", "zh", "c"))
    mine = lax.dynamic_slice_in_dim(weight, x * 32, 32, 0)
    near = exchanged(mine, "zh", 1)

    own, oth = local_grads(c[None], hidden, out_grad, e1.T)
    got = shifted(after(oth, near), "c", 1)
    pairs = paired(own, got)
    columns = swap(pairs, "y")
    two = jnp.stack([mine, after(near, pairs)])
    quarter = jnp.concatenate([two, exchanged(two, "zh", 3)])

    line = lined(columns)
    again = requantized(swap(after(line, quarter), "zh"), e2.T)
    rows = swap(again.reshape(N_OUTER, -1, 256), OUTER)

    part = jnp.stack(pieces(after(quarter, line), "x"))
    part = jnp.stack([after(piece, again) for piece in pieces(part, "y")])
    pos = jnp.stack([c, x, y, zh])
    hidden_grad = hidden_grads(pos, out_grad, part, shifted(part, "c", 1))
    return hidden_grad, summed(after(rows, hidden_grad))


def solution(mesh):
    fine = Mesh(mesh.devices.reshape(tuple(SIZES.values())), AXES)
    every, inner = P(AXES, None), ("y", "zh", "c")
    return jax.shard_map(
        per_device,
        mesh=fine,
        in_specs=(every, every, P(None, inner), every, P(OUTER, inner)),
        out_specs=(every, P(OUTER, inner)),
        check_vma=False,
    )
```

```python
import jax
import jax.numpy as jnp
from jax import lax
from jax.experimental import pallas as pl
from jax.experimental.pallas import tpu as pltpu
from jax.sharding import Mesh, PartitionSpec as P

SIZES = {"x": 4, "zl": 8, "y": 4, "zh": 4, "c": 2}
AXES = tuple(SIZES)
OUTER = ("x", "zl")
N_OUTER = 32
LIMIT = 448.0
VMEM = 3 << 20
VMEM_LOCAL, VMEM_HIDDEN = 3 << 20, 65_500_000
ORDER = (0, 1, 3, 2)
F32, BF16 = jnp.float32, jnp.bfloat16


def limits(exponent):
    return jnp.left_shift(1, exponent + 16).astype(F32) * (LIMIT * 2.0**-16)


def grad_kernel(core, hid, og, exponent, own, oth, acts):
    c = core[0]

    @pl.when(pl.program_id(0) == 0)
    def _():
        acts[...] = hid[...].T

    bound = limits(exponent[...])
    other = pltpu.roll(bound, 14, 0)
    for side, out in ((c, own), (1 - c, oth)):
        mine = jnp.where(side == 0, bound, other).T
        for zh in range(4):
            cols = og[:, pl.ds(pl.multiple_of(512 * zh + 256 * side, 256), 256)]
            local = jnp.dot(acts[...], cols, preferred_element_type=F32)
            for half in range(2):
                most = mine[:, 4 * zh + half : 4 * zh + half + 1]
                lanes = slice(128 * half, 128 * half + 128)
                out[zh, :, lanes] = jnp.clip(local[:, lanes], -most, most).astype(BF16)


def local_grads(core, hidden, out_grad, exponent):
    block = jax.ShapeDtypeStruct((16, 128, 256), BF16)
    return pl.pallas_call(
        grad_kernel,
        grid_spec=pltpu.PrefetchScalarGridSpec(
            num_scalar_prefetch=1,
            grid=(4,),
            in_specs=[
                pl.BlockSpec((192, 128), lambda y, core: (0, 0)),
                pl.BlockSpec((192, 2048), lambda y, core: (0, y)),
                pl.BlockSpec((16, 128), lambda y, core: (y, 0)),
            ],
            out_specs=[pl.BlockSpec((4, 128, 256), lambda y, core: (y, 0, 0))] * 2,
            scratch_shapes=[pltpu.VMEM((128, 192), BF16)],
        ),
        out_shape=[block, block],
        compiler_params=pltpu.CompilerParams(vmem_limit_bytes=VMEM_LOCAL),
        cost_estimate=pl.CostEstimate(flops=1 << 20, bytes_accessed=1 << 16, transcendentals=0),
        name="local_grads",
    )(core, hidden, out_grad, exponent)


def pair_kernel(own, got, out):
    out[...] = (own[...].astype(F32) + got[...].astype(F32)).astype(BF16)


def paired(own, got):
    block = pl.BlockSpec((4, 128, 256), lambda y: (y, 0, 0))
    return pl.pallas_call(
        pair_kernel,
        grid=(4,),
        in_specs=[block, block],
        out_specs=block,
        out_shape=jax.ShapeDtypeStruct((16, 128, 256), BF16),
        compiler_params=pltpu.CompilerParams(vmem_limit_bytes=VMEM),
        cost_estimate=pl.CostEstimate(flops=1 << 20, bytes_accessed=3 << 20, transcendentals=0),
        name="paired",
    )(own, got).reshape(4, 4, 128, 256)


def hidden_kernel(pos, og, own, oth, out, total):
    c, x, zh = pos[0], pos[1], pos[3]
    step = pl.program_id(0)

    @pl.when(step == 0)
    def _():
        total[...] = jnp.zeros_like(total)

    acc = total[...]
    for k, bits in enumerate(ORDER):
        for core, part in ((c, own), (1 - c, oth)):
            rows = part[0, :, k].reshape(128, 256)
            at = pl.multiple_of(512 * jnp.bitwise_xor(zh, bits) + core * 256, 256)
            acc += lax.dot_general(og[:, pl.ds(at, 256)], rows, (((1,), (1,)), ((), ())), preferred_element_type=F32)
    total[...] = acc

    @pl.when(step == 3)
    def _():
        out[...] = pltpu.roll(acc, 32 * x, 1).astype(BF16)


def hidden_grads(pos, out_grad, own, oth):
    part = pl.BlockSpec((1, 4, 4, 32, 256), lambda k, pos: (k, 0, 0, 0, 0))
    return pl.pallas_call(
        hidden_kernel,
        grid_spec=pltpu.PrefetchScalarGridSpec(
            num_scalar_prefetch=1,
            grid=(4,),
            in_specs=[pl.BlockSpec((192, 2048), lambda k, pos: (0, lax.rem(pos[2] + k, 4))), part, part],
            out_specs=pl.BlockSpec((192, 128), lambda k, pos: (0, 0)),
            scratch_shapes=[pltpu.VMEM((192, 128), F32)],
        ),
        out_shape=jax.ShapeDtypeStruct((192, 128), BF16),
        compiler_params=pltpu.CompilerParams(vmem_limit_bytes=VMEM_HIDDEN),
        cost_estimate=pl.CostEstimate(flops=2 * 192 * 128 * 8192, bytes_accessed=5 << 20, transcendentals=0),
        name="hidden_grads",
    )(pos, out_grad, own, oth)


def line_kernel(parts, out):
    out[0] = parts[:, 0].astype(F32).sum(0).astype(BF16)


def lined(parts):
    return pl.pallas_call(
        line_kernel,
        grid=(4,),
        in_specs=[pl.BlockSpec((4, 1, 128, 256), lambda zh: (0, zh, 0, 0))],
        out_specs=pl.BlockSpec((1, 128, 256), lambda zh: (zh, 0, 0)),
        out_shape=jax.ShapeDtypeStruct((4, 128, 256), BF16),
        compiler_params=pltpu.CompilerParams(vmem_limit_bytes=VMEM),
        cost_estimate=pl.CostEstimate(flops=1 << 19, bytes_accessed=5 << 18, transcendentals=0),
        name="lined",
    )(parts)


def again_kernel(parts, exponent, out):
    bound = limits(exponent[...]).T
    for half in range(2):
        lanes = slice(128 * half, 128 * half + 128)
        group = parts[:, :, lanes].astype(F32).sum(0)
        most = bound[:, half : half + 1]
        out[:, lanes] = jnp.clip(group, -most, most).astype(BF16)


def requantized(parts, exponent):
    return pl.pallas_call(
        again_kernel,
        out_shape=jax.ShapeDtypeStruct((128, 256), BF16),
        compiler_params=pltpu.CompilerParams(vmem_limit_bytes=VMEM),
        cost_estimate=pl.CostEstimate(flops=1 << 17, bytes_accessed=5 << 16, transcendentals=0),
        name="requantized",
    )(parts, exponent)


def exchanged(value, axis, bits):
    return lax.ppermute(value, axis, [(i, i ^ bits) for i in range(SIZES[axis])])


def shifted(value, axis, k):
    n = SIZES[axis]
    return lax.ppermute(value, axis, [(i, (i - k) % n) for i in range(n)])


def pieces(value, axis):
    return [value] + [shifted(value, axis, k) for k in (1, 2, 3)]


def swap(value, axes):
    return lax.all_to_all(value, axes, 0, 0, tiled=True)


def after(value, *earlier):
    return lax.optimization_barrier((value, *earlier))[0]


def summed(parts):
    return parts.astype(F32).sum(0)


def per_device(out_grad, hidden, weight, e1, e2):
    x, y, zh, c = (lax.axis_index(a) for a in ("x", "y", "zh", "c"))
    mine = lax.dynamic_slice_in_dim(weight, x * 32, 32, 0)
    near = exchanged(mine, "zh", 1)

    own, oth = local_grads(c[None], hidden, out_grad, e1.T)
    got = shifted(after(oth, near), "c", 1)
    pairs = paired(own, got)
    columns = swap(pairs, "y")
    two = jnp.stack([mine, after(near, pairs)])
    quarter = jnp.concatenate([two, exchanged(two, "zh", 3)])

    line = lined(columns)
    again = requantized(swap(after(line, quarter), "zh"), e2.T)
    rows = swap(again.reshape(N_OUTER, -1, 256), OUTER)

    part = jnp.stack(pieces(after(quarter, line), "x"))
    part = jnp.stack([after(piece, again) for piece in pieces(part, "y")])
    pos = jnp.stack([c, x, y, zh])
    hidden_grad = hidden_grads(pos, out_grad, part, shifted(part, "c", 1))
    return hidden_grad, summed(after(rows, hidden_grad))


def solution(mesh):
    fine = Mesh(mesh.devices.reshape(tuple(SIZES.values())), AXES)
    every, inner = P(AXES, None), ("y", "zh", "c")
    return jax.shard_map(
        per_device,
        mesh=fine,
        in_specs=(every, every, P(None, inner), every, P(OUTER, inner)),
        out_specs=(every, P(OUTER, inner)),
        check_vma=False,
    )
```
